32 devices in a mesh: grp: 2 (over x), freq: 8 (over z, y), rcv: 2 (over core).
Axes of the slice: x: 2, y: 2, z: 4, core: 2. Of those that a mesh axis runs over, the one named last changes fastest.
Arguments:
- kernel: bfloat16 [8, 2, 2048, 2048], P('freq', None, None, 'rcv'), may hold values from -0.09375 to 0.09375
- focus: bfloat16 [2048, 256, 256], P(('rcv', 'freq'), 'grp'), parts along dimension 1, may hold values from -6 to 6
- onset: int32 [2048, 256], P(None, 'grp'), parts along dimension 1, may hold values from 16 to 127
Outputs:
- updated: bfloat16 [2048, 256, 256], P(('rcv', 'freq'), 'grp'), parts along dimension 1
The draws below stay inside these ranges and needn't reach their ends.
There are 2 independent parts, one for each index of `grp`. The reference program is written for one: setup_inputs(seed, part) draws one part's arguments, and reference() takes and returns one part's arrays. A program takes and returns all parts, laid end to end along the dimension named above; an argument that names none is the same for every part. Nothing has to cross between parts.
Inputs may be any that keep to these rules, and one draw needn't show every extreme that they name: onset is the direct-arrival time of focal point p at surface point x, in samples.
All inputs are finite; a program needn't handle non-finite values.
Results may differ from the reference program's by a relative error of at most 0.0028.
Values may be sent and summed in bfloat16 or wider, within the bound.
A program may use at most 128 MiB of HBM per device.

```python
import math
import jax
import jax.numpy as jnp
from jax import lax

POINTS = 2048
NT = 256
P_GRP = 128
NF = 8


def with_ends(drawn, key, least, largest):
    index_at = [jax.random.randint(jax.random.fold_in(key, axis), (), 0, length) for axis, length in enumerate(drawn.shape)]
    widest = drawn.shape.index(max(drawn.shape))
    beside = index_at[:widest] + [(index_at[widest] + 1) % drawn.shape[widest]] + index_at[widest + 1:]
    return drawn.at[tuple(index_at)].set(least).at[tuple(beside)].set(largest)


def block_levels(rng, extent, shards, smallest, largest):
    gain, own = 1.0, jax.random.fold_in(rng, 6)
    for dim, shards_of in shards:
        heights = jnp.exp(jax.random.uniform(jax.random.fold_in(own, dim), (shards_of,), jnp.float32, smallest / len(shards), largest / len(shards)))
        gain = gain * jnp.repeat(heights, extent[dim] // shards_of).reshape([-1 if axis == dim else 1 for axis in range(len(extent))])
    return gain


def bell_draw(own_key, dims, deviation, reach, pieces=(), kind=jnp.bfloat16):
    level = block_levels(own_key, dims, pieces, -0.22, 0.18) if pieces else 1.0
    values = jax.random.normal(own_key, dims, jnp.float32) * deviation * level
    return jnp.minimum(jnp.maximum(values, -reach), reach).astype(kind)


def setup_inputs(seed: int = 0, part: int = 0) -> dict:
    key_of = jax.random.split(jax.random.key(seed), 4)
    own_keys = jax.random.split(jax.random.fold_in(key_of[3], part), 4)
    kernel = bell_draw(key_of[0], (NF, 2, POINTS, POINTS), (2 * POINTS) ** -0.5, 0.09375, ((0, 8), (3, 2)))
    focus = bell_draw(own_keys[1], (POINTS, P_GRP, NT), 1.0, 6.0, ((0, 16),))
    onset = with_ends(jax.random.randint(own_keys[2], (POINTS, P_GRP), NT // 16, NT // 2), jax.random.fold_in(own_keys[2], 1), NT // 16, (NT // 2) - 1).astype(jnp.int32)
    return {"kernel": kernel, "focus": focus, "onset": onset}


def tables(nt, nf):
    sample_count = jnp.arange(nt, dtype=jnp.int32)
    bins = jnp.arange(nf, dtype=jnp.int32) + 1
    phase = ((bins[:, None] * sample_count[None, :]) % nt).astype(jnp.float32) * (2.0 * math.pi / nt)
    forward = jnp.stack([jnp.cos(phase), -jnp.sin(phase)], axis=1)
    return forward, forward * (2.0 / nt)


def taper_window(onset_rows, nt):
    sample_count = jnp.arange(nt, dtype=jnp.int32)
    edge = onset_rows[:, :, None]
    keep = (sample_count[None, None, :] < edge) | (sample_count[None, None, :] > nt - edge)
    return jnp.where(keep, 1.0, 0.0).astype(jnp.float32)


def plain_dot(left_operand, right_operand):
    return jnp.dot(left_operand, right_operand, preferred_element_type=jnp.float32)


def left_dot(left_operand, right_operand):
    return lax.dot_general(left_operand, right_operand, (((0,), (0,)), ((), ())), preferred_element_type=jnp.float32)


def reference(kernel, focus, onset):
    highest = lax.Precision.HIGHEST
    forward, inverse = tables(NT, NF)
    mask = taper_window(onset, NT)
    spec = jnp.einsum('xpt,fct->fcxp', focus.astype(jnp.float32), forward, precision=highest).astype(jnp.bfloat16)

    def convolve(pair):
        slab, field = pair
        real_part = plain_dot(slab[0], field[0]) - plain_dot(slab[1], field[1])
        imag_part = plain_dot(slab[0], field[1]) + plain_dot(slab[1], field[0])
        return jnp.stack([real_part, imag_part]).astype(jnp.bfloat16)

    gspec = lax.map(convolve, (kernel, spec))
    minus = jnp.einsum('fcxp,fct->xpt', gspec.astype(jnp.float32), inverse, precision=highest) * mask
    mspec = jnp.einsum('xpt,fct->fcxp', minus, forward, precision=highest).astype(jnp.bfloat16)

    def correlate(pair):
        slab, field = pair
        real_part = left_dot(slab[0], field[0]) + left_dot(slab[1], field[1])
        imag_part = left_dot(slab[0], field[1]) - left_dot(slab[1], field[0])
        return jnp.stack([real_part, imag_part]).astype(jnp.bfloat16)

    hspec = lax.map(correlate, (kernel, mspec))
    update = jnp.einsum('fcxp,fct->xpt', hspec.astype(jnp.float32), inverse, precision=highest) * mask
    return (focus.astype(jnp.float32) + update).astype(jnp.bfloat16)
```

```python
import functools
import math

import jax
import jax.numpy as jnp
import numpy as np
from jax import lax
from jax.experimental import pallas as pl
from jax.experimental.pallas import tpu as pltpu
from jax.sharding import PartitionSpec as P

MESH = pl.DeviceIdType.MESH
NSUB = 2
BF = jnp.bfloat16
F32 = jnp.float32


def forward_table(nt, nf):
    phase = ((np.arange(1, nf + 1)[:, None] * np.arange(nt)[None, :]) % nt) * (2.0 * math.pi / nt)
    return np.stack([np.cos(phase), -np.sin(phase)], axis=1).reshape(2 * nf, nt).astype(np.float32)


def split(table):
    high = table.astype(jnp.bfloat16)
    low = (table - high.astype(np.float32)).astype(jnp.bfloat16)
    return high, low


def dot(a, b, dims):
    return lax.dot_general(a, b, (dims, ((), ())), preferred_element_type=F32)


def spectra_kernel(
    nf, rows, np_, nt, kern_hbm, foc_hbm, ons_ref, tab_ref, out_hbm,
    kern_v, foc_v, spec_f, spec_s, spec_r, acc, part_s, part_r, g_s, g_r, g_f, dk,
    m_s, m_r, m_o, acc2, h_s,
    load_sem, s1, r1, sp, rp, s2, r2, s3, r3, so, ro, s4, r4,
):
    me = lax.axis_index("freq")
    core = lax.axis_index("rcv")
    nk = 2 * nf
    half = nf * rows
    sub = rows // NSUB
    per = max(1, 128 // rows)
    chunk = per * rows
    nch = half // chunk

    def dest_of(d):
        return lax.rem(me - d + nf, nf)

    def src_of(d):
        return lax.rem(me + d, nf)

    def peer(src, dst, ssem, rsem, dest):
        return pltpu.make_async_remote_copy(
            src_ref=src, dst_ref=dst, send_sem=ssem, recv_sem=rsem,
            device_id={"freq": dest}, device_id_type=MESH)

    def mate(src, dst, ssem, rsem):
        return pltpu.make_async_remote_copy(
            src_ref=src, dst_ref=dst, send_sem=ssem, recv_sem=rsem,
            device_id={"rcv": 1 - core}, device_id_type=MESH)

    def c1(d, b):
        w = pl.ds(b * sub, sub)
        return peer(spec_s.at[dest_of(d), :, w], spec_r.at[me, :, w], s1.at[b, d], r1.at[b, d], dest_of(d))

    def cp(d):
        return mate(part_s.at[d], part_r.at[d], sp.at[d], rp.at[d])

    def c2(d):
        return peer(g_s.at[dest_of(d)], g_r.at[me], s2.at[d], r2.at[d], dest_of(d))

    def c3(d):
        return peer(m_s.at[dest_of(d)], m_r.at[me], s3.at[d], r3.at[d], dest_of(d))

    def co(d):
        return mate(m_r.at[src_of(d)], m_o.at[src_of(d)], so.at[d], ro.at[d])

    def c4(d):
        return peer(h_s.at[dest_of(d)], out_hbm.at[me], s4.at[d], r4.at[d], dest_of(d))

    loads = [pltpu.make_async_copy(foc_hbm.at[pl.ds(b * sub, sub)], foc_v.at[pl.ds(b * sub, sub)], load_sem.at[b])
             for b in range(NSUB)]
    kload = pltpu.make_async_copy(kern_hbm.at[0], kern_v, load_sem.at[NSUB])
    for load in loads:
        load.start()
    kload.start()

    barrier = pltpu.get_barrier_semaphore()

    @pl.loop(1, nf)
    def _(d):
        pl.semaphore_signal(barrier, inc=1, device_id={"freq": dest_of(d)}, device_id_type=MESH)

    pl.semaphore_signal(barrier, inc=1, device_id={"rcv": 1 - core}, device_id_type=MESH)

    for b in range(NSUB):
        loads[b].wait()

        @pl.loop(0, sub // 2, unroll=4)
        def _(i):
            x = b * sub + 2 * i
            f = foc_v[pl.ds(x, 2)].reshape(2 * np_, nt)
            s = dot(tab_ref[...], f, ((1,), (1,)))
            s = s[:nk] + s[nk:]
            spec_f[pl.ds(x * nk, nk), :] = s[:, :np_]
            spec_f[pl.ds((x + 1) * nk, nk), :] = s[:, np_:]

        for k in range(nk):
            v = spec_f[pl.ds(b * sub * nk + k, sub, stride=nk), :]
            spec_s[k // 2, k % 2, pl.ds(b * sub, sub), :] = v.astype(BF)
        if b == 0:
            pl.semaphore_wait(barrier, nf)

        @pl.loop(1, nf)
        def _(d):
            c1(d, b).start()

    spec_r[me] = spec_s[me]

    theta = (ons_ref[...].astype(F32) - 0.5) * (2.0 * math.pi / nt)
    c_1, s_1 = jnp.cos(theta), jnp.sin(theta)
    dk[nf - 1] = (2.0 * ons_ref[...].astype(F32) - 1.0) * (1.0 / nt)
    cm, sm = c_1, s_1
    for m in range(1, 2 * nf + 1):
        value = sm * (1.0 / (nt * math.sin(math.pi * m / nt)))
        dk[nf - 1 + m] = value
        if m < nf:
            dk[nf - 1 - m] = value
        cm, sm = cm * c_1 - sm * s_1, sm * c_1 + cm * s_1

    acc[...] = jnp.zeros_like(acc)
    kload.wait()

    q0 = me // per

    def get_rhs(step):
        q = lax.rem(q0 + step, nch)

        @pl.loop(0, per)
        def _(j):
            d = lax.rem(q * per + j - me + nf, nf)

            @pl.when(d != 0)
            def _():
                for b in range(NSUB):
                    c1(d, b).wait_recv()

        s = spec_r[pl.ds(q * per, per)]
        re = s[:, 0].reshape(chunk, np_)
        im = s[:, 1].reshape(chunk, np_)
        rhs = jnp.concatenate(
            [jnp.concatenate([re, im], 1), jnp.concatenate([-im, re], 1)], 0)
        return pl.multiple_of(q * chunk, chunk), rhs

    tile = min(512, half)

    @pl.loop(0, nch - 1)
    def _(step):
        j, rhs = get_rhs(step)

        @pl.loop(0, 2 * half // tile)
        def _(t):
            w = pl.ds(pl.multiple_of(t * tile, tile), tile)
            lhs = jnp.concatenate([kern_v[0, w, pl.ds(j, chunk)], kern_v[1, w, pl.ds(j, chunk)]], 1)
            acc[w, :] += dot(lhs, rhs, ((1,), (0,)))

    j_last, rhs_last = get_rhs(nch - 1)

    def last(row):
        w = pl.ds(pl.multiple_of(row, rows), rows)
        lhs = jnp.concatenate([kern_v[0, w, pl.ds(j_last, chunk)], kern_v[1, w, pl.ds(j_last, chunk)]], 1)
        return acc[w, :] + dot(lhs, rhs_last, ((1,), (0,)))

    @pl.loop(1, nf + 1)
    def _(e):
        d = lax.rem(e, nf)
        part_s[d] = last((1 - core) * half + dest_of(d) * rows).astype(BF)
        cp(d).start()

    @pl.loop(1, nf + 1)
    def _(e):
        d = lax.rem(e, nf)
        own = last(core * half + dest_of(d) * rows)
        cp(d).wait_recv()
        g = (own + part_r[d].astype(F32)).astype(BF)
        g_s[dest_of(d), 0] = g[:, :np_]
        g_s[dest_of(d), 1] = g[:, np_:]

        @pl.when(d != 0)
        def _():
            c2(d).start()

    g_f[me] = g_s[me].astype(F32)

    @pl.loop(1, nf)
    def _(d):
        c2(d).wait_recv()
        g_f[src_of(d)] = g_r[src_of(d)].astype(F32)

    @pl.loop(1, nf + 1)
    def _(e):
        d = lax.rem(e, nf)
        a = dest_of(d)

        @pl.loop(0, rows // 16)
        def _(t):
            w = pl.ds(pl.multiple_of(t * 16, 16), 16)
            re = jnp.zeros((16, np_), F32)
            im = jnp.zeros((16, np_), F32)
            for f in range(nf):
                lo = dk[a - f + nf - 1, w, :]
                hi = dk[a + f + nf + 1, w, :]
                re = re + (lo + hi) * g_f[f, 0, w, :]
                im = im + (lo - hi) * g_f[f, 1, w, :]
            m_s[a, 0, w, :] = re.astype(BF)
            m_s[a, 1, w, :] = im.astype(BF)

        @pl.when(d != 0)
        def _():
            c3(d).start()

    m_r[me] = m_s[me]
    acc2[...] = jnp.zeros_like(acc2)

    def adjoint(buf, owner, src):
        mr, mi = buf[src, 0], buf[src, 1]
        lhs = jnp.concatenate(
            [jnp.concatenate([mr, mi], 1), jnp.concatenate([mi, -mr], 1)], 0)
        w = pl.ds(pl.multiple_of(owner * half + src * rows, rows), rows)
        rhs = jnp.concatenate([kern_v[0, w, :], kern_v[1, w, :]], 0)
        acc2[...] += dot(lhs, rhs, ((0,), (0,)))

    @pl.loop(0, nf)
    def _(d):
        @pl.when(d != 0)
        def _():
            c3(d).wait_recv()

        co(d).start()
        adjoint(m_r, core, src_of(d))

        @pl.when(d != 0)
        def _():
            co(d - 1).wait_recv()
            adjoint(m_o, 1 - core, src_of(d - 1))

    co(nf - 1).wait_recv()
    adjoint(m_o, 1 - core, src_of(nf - 1))

    @pl.loop(1, nch + 1)
    def _(e):
        q = lax.rem(q0 - e + 2 * nch, nch)
        w = pl.ds(pl.multiple_of(q * chunk, chunk), chunk)
        for c in range(2):
            t = jnp.swapaxes(acc2[pl.ds(c * np_, np_), w], 0, 1).astype(BF)
            h_s[pl.ds(q * per, per), c] = t.reshape(per, rows, np_)

        @pl.loop(0, per)
        def _(j):
            d = lax.rem(me - (q * per + j) + nf, nf)

            @pl.when(d != 0)
            def _():
                c4(d).start()

    keep = pltpu.make_async_copy(h_s.at[me], out_hbm.at[me], load_sem.at[0])
    keep.start()

    @pl.loop(1, nf)
    def _(d):
        c4(d).wait_recv()

    @pl.loop(1, nf)
    def _(d):
        for b in range(NSUB):
            c1(d, b).wait_send()
        c2(d).wait_send()
        c3(d).wait_send()
        c4(d).wait_send()

    @pl.loop(0, nf)
    def _(d):
        cp(d).wait_send()
        co(d).wait_send()

    keep.wait()


def final_kernel(nf, step_rows, np_, nt, h_ref, ons_ref, foc_ref, tab_ref, out_ref, rows_f):
    nk = 2 * nf
    width = nk + 16
    for k in range(nk):
        rows_f[pl.ds(k, step_rows, stride=width), :] = h_ref[k // 2, k % 2].astype(F32)
    rows_f[pl.ds(nk, step_rows, stride=width), :] = ons_ref[...].astype(F32)
    for k in range(nk + 1, width):
        rows_f[pl.ds(k, step_rows, stride=width), :] = jnp.full((step_rows, np_), 1.0 if k == nk + 1 else 0.0, F32)
    for x in range(step_rows):
        r = rows_f[pl.ds(x * width, width), :].astype(BF)
        lhs = jnp.concatenate([r[:nk], r], 0)
        both = dot(lhs, tab_ref[...], ((0,), (0,)))
        f = foc_ref[x].astype(F32)
        out_ref[x] = (f + jnp.where(both[:, nt:] > 0.0, both[:, :nt], 0.0)).astype(BF)


def shards(kernel, focus, onset):
    nf = lax.axis_size("freq")
    rows, np_, nt = focus.shape
    half = nf * rows
    start = (lax.axis_index("rcv") * nf + lax.axis_index("freq")) * rows
    own = lax.dynamic_slice_in_dim(onset, start, rows, 0)
    table = forward_table(nt, nf)
    fwd = jnp.asarray(np.concatenate(split(table), 0))
    inv_hi, inv_lo = split((table * np.float32(2.0 / nt)).astype(np.float32))
    nk = 2 * nf
    t = np.arange(nt)
    right = np.zeros((2 * nk + 16, 2 * nt), np.float32).astype(jnp.bfloat16)
    right[:nk, :nt] = inv_hi
    right[nk:2 * nk, :nt] = inv_lo
    right[2 * nk, nt:] = 1.0
    right[2 * nk + 1, nt:] = -np.minimum(t, nt - t)
    right = jnp.asarray(right)

    def vm(shape, kind=BF):
        return pltpu.VMEM(shape, kind)

    block = (nf, 2, rows, np_)
    dma = pltpu.SemaphoreType.DMA
    spectra = pl.pallas_call(
        functools.partial(spectra_kernel, nf, rows, np_, nt),
        out_shape=jax.ShapeDtypeStruct(block, BF),
        in_specs=[pl.BlockSpec(memory_space=pl.ANY)] * 2 + [pl.BlockSpec(memory_space=pltpu.VMEM)] * 2,
        out_specs=pl.BlockSpec(memory_space=pl.ANY),
        scratch_shapes=[
            vm((2, 2 * half, half)), vm((rows, np_, nt)), vm((rows * nk, np_), F32),
            vm(block), vm(block), vm((2 * half, 2 * np_), F32),
            vm((nf, rows, 2 * np_)), vm((nf, rows, 2 * np_)),
            vm(block), vm(block), vm(block, F32), vm((3 * nf, rows, np_), F32),
            vm(block), vm(block), vm(block), vm((2 * np_, half), F32), vm(block),
            dma((NSUB + 1,)), dma((NSUB, nf)), dma((NSUB, nf)),
        ] + [dma((nf,))] * 10,
        compiler_params=pltpu.CompilerParams(
            collective_id=0, has_side_effects=True, vmem_limit_bytes=56 << 20),
        cost_estimate=pl.CostEstimate(
            flops=32 * half * half * np_, bytes_accessed=8 * half * half, transcendentals=0),
    )(kernel, focus, own, fwd)
    sr = 16
    return pl.pallas_call(
        functools.partial(final_kernel, nf, sr, np_, nt),
        out_shape=jax.ShapeDtypeStruct(focus.shape, BF),
        grid=(rows // sr,),
        in_specs=[
            pl.BlockSpec((nf, 2, sr, np_), lambda i: (0, 0, i, 0)),
            pl.BlockSpec((sr, np_), lambda i: (i, 0)),
            pl.BlockSpec((sr, np_, nt), lambda i: (i, 0, 0)),
            pl.BlockSpec(right.shape, lambda i: (0, 0)),
        ],
        out_specs=pl.BlockSpec((sr, np_, nt), lambda i: (i, 0, 0)),
        scratch_shapes=[pltpu.VMEM((sr * (nk + 16), np_), F32)],
        compiler_params=pltpu.CompilerParams(vmem_limit_bytes=32 << 20),
    )(spectra, own, focus, right)


def solution(mesh):
    in_specs = (P("freq", None, None, "rcv"), P(("rcv", "freq"), "grp", None), P(None, "grp"))
    out_specs = P(("rcv", "freq"), "grp", None)
    return jax.shard_map(shards, mesh=mesh, in_specs=in_specs, out_specs=out_specs, check_vma=False)
```

```python
import functools
import math

import jax
import jax.numpy as jnp
import numpy as np
from jax import lax
from jax.experimental import pallas as pl
from jax.experimental.pallas import tpu as pltpu
from jax.sharding import PartitionSpec as P

MESH = pl.DeviceIdType.MESH
NSUB = 2
BF = jnp.bfloat16
F32 = jnp.float32


def forward_table(nt, nf):
    phase = ((np.arange(1, nf + 1)[:, None] * np.arange(nt)[None, :]) % nt) * (2.0 * math.pi / nt)
    return np.stack([np.cos(phase), -np.sin(phase)], axis=1).reshape(2 * nf, nt).astype(np.float32)


def split(table):
    high = table.astype(jnp.bfloat16)
    low = (table - high.astype(np.float32)).astype(jnp.bfloat16)
    return high, low


def dot(a, b, dims):
    return lax.dot_general(a, b, (dims, ((), ())), preferred_element_type=F32)


def swap(block, first):
    h = block.shape[1] // 2
    re, im = block[:, :h], block[:, h:]
    return jnp.concatenate([-im, re] if first else [im, -re], 1)


def spectra_kernel(
    nf, rows, np_, nt, kern_hbm, foc_hbm, ons_hbm, tab_ref, out_hbm, ons_out,
    kern_v, foc_v, ons_v, spec_f, spec_s, spec_r, acc, part_s, part_r, g_s, g_r, g_f, dk,
    m_s, m_r, m_o, acc2, h_s,
    load_sem, s1, r1, sp, rp, s2, r2, s3, r3, so, ro, s4, r4,
):
    me = lax.axis_index("freq")
    core = lax.axis_index("rcv")
    nk = 2 * nf
    ph = np_ // 2
    half = nf * rows
    sub = rows // NSUB
    per = max(1, 128 // rows)
    chunk = per * rows
    nch = half // chunk
    nd = 2 * nf - 1

    def dest_of(d):
        return lax.rem(me - d + nf, nf)

    def src_of(d):
        return lax.rem(me + d, nf)

    def peer(src, dst, ssem, rsem, dest):
        return pltpu.make_async_remote_copy(
            src_ref=src, dst_ref=dst, send_sem=ssem, recv_sem=rsem,
            device_id={"freq": dest}, device_id_type=MESH)

    def mate(src, dst, ssem, rsem):
        return pltpu.make_async_remote_copy(
            src_ref=src, dst_ref=dst, send_sem=ssem, recv_sem=rsem,
            device_id={"rcv": 1 - core}, device_id_type=MESH)

    def c1(d, h, b):
        w = pl.ds(b * sub, sub) if h == 0 else pl.ds(0, rows)
        i = b if h == 0 else NSUB
        return peer(spec_s.at[h, dest_of(d), w], spec_r.at[h, me, w], s1.at[i, d], r1.at[i, d], dest_of(d))

    def cp(d, h):
        return mate(part_s.at[h, d], part_r.at[h, d], sp.at[h, d], rp.at[h, d])

    def c2(d, h):
        return peer(g_s.at[h, dest_of(d)], g_r.at[h, me], s2.at[h, d], r2.at[h, d], dest_of(d))

    def c3(d, h):
        return peer(m_s.at[h, dest_of(d)], m_r.at[h, me], s3.at[h, d], r3.at[h, d], dest_of(d))

    def co(d, h):
        return mate(m_r.at[h, src_of(d)], m_o.at[h, src_of(d)], so.at[h, d], ro.at[h, d])

    def c4(d, h):
        return peer(h_s.at[h, dest_of(d)], out_hbm.at[h, me], s4.at[h, d], r4.at[h, d], dest_of(d))

    loads = [pltpu.make_async_copy(foc_hbm.at[pl.ds(b * sub, sub)], foc_v.at[pl.ds(b * sub, sub)], load_sem.at[b])
             for b in range(NSUB)]
    kload = pltpu.make_async_copy(kern_hbm.at[0], kern_v, load_sem.at[NSUB])
    oload = pltpu.make_async_copy(
        ons_hbm.at[pl.ds(pl.multiple_of((core * nf + me) * rows, rows), rows)], ons_v, load_sem.at[NSUB + 1])
    for load in loads:
        load.start()
    oload.start()
    kload.start()

    barrier = pltpu.get_barrier_semaphore()

    @pl.loop(1, nf)
    def _(d):
        pl.semaphore_signal(barrier, inc=1, device_id={"freq": dest_of(d)}, device_id_type=MESH)

    pl.semaphore_signal(barrier, inc=1, device_id={"rcv": 1 - core}, device_id_type=MESH)

    for b in range(NSUB):
        loads[b].wait()

        @pl.loop(0, sub // 2, unroll=4)
        def _(i):
            x = b * sub + 2 * i
            f = foc_v[pl.ds(x, 2)].reshape(2 * np_, nt)
            s = dot(tab_ref[...], f, ((1,), (1,)))
            s = s[:nk] + s[nk:]
            for y in range(2):
                for h in range(2):
                    lo = y * np_ + h * ph
                    spec_f[h, pl.ds((x + y) * nf, nf), :] = jnp.concatenate(
                        [s[:nf, lo:lo + ph], s[nf:, lo:lo + ph]], 1)

        for h in range(2):
            for k in range(nf):
                v = spec_f[h, pl.ds(b * sub * nf + k, sub, stride=nf), :]
                spec_s[h, k, pl.ds(b * sub, sub), :] = v.astype(BF)
            if h == 0:
                if b == 0:
                    pl.semaphore_wait(barrier, nf)

                @pl.loop(1, nf)
                def _(d):
                    c1(d, 0, b).start()

    @pl.loop(1, nf)
    def _(d):
        c1(d, 1, 0).start()

    for h in range(2):
        spec_r[h, me] = spec_s[h, me]

    oload.wait()
    okeep = pltpu.make_async_copy(ons_v, ons_out, load_sem.at[NSUB + 1])
    okeep.start()
    real = lax.broadcasted_iota(jnp.int32, (rows, np_), 1) < ph
    for h in range(2):
        on = ons_v[:, h * ph:(h + 1) * ph].astype(F32)
        on = jnp.concatenate([on, on], 1)
        theta = (on - 0.5) * (2.0 * math.pi / nt)
        c_1, s_1 = jnp.cos(theta), jnp.sin(theta)
        dk[h, nf - 1] = (2.0 * on - 1.0) * (1.0 / nt)
        cm, sm = c_1, s_1
        for m in range(1, 2 * nf + 1):
            value = sm * (1.0 / (nt * math.sin(math.pi * m / nt)))
            if m < nf:
                dk[h, nf - 1 + m] = value
                dk[h, nf - 1 - m] = value
            if m > 1:
                dk[h, nd + m - 2] = jnp.where(real, value, -value)
            cm, sm = cm * c_1 - sm * s_1, sm * c_1 + cm * s_1

    acc[...] = jnp.zeros_like(acc)
    acc2[...] = jnp.zeros_like(acc2)
    kload.wait()

    q0 = me // per
    tile = min(512, half)

    def forward_product(h):
        def get_rhs(step):
            q = lax.rem(q0 + step, nch)

            @pl.loop(0, per)
            def _(j):
                d = lax.rem(q * per + j - me + nf, nf)

                @pl.when(d != 0)
                def _():
                    for b in range(NSUB if h == 0 else 1):
                        c1(d, h, b).wait_recv()

            s = spec_r[h, pl.ds(q * per, per)].reshape(chunk, np_)
            return pl.multiple_of(q * chunk, chunk), jnp.concatenate([s, swap(s, True)], 0)

        @pl.loop(0, nch - 1)
        def _(step):
            j, rhs = get_rhs(step)

            @pl.loop(0, 2 * half // tile)
            def _(t):
                w = pl.ds(pl.multiple_of(t * tile, tile), tile)
                lhs = jnp.concatenate([kern_v[0, w, pl.ds(j, chunk)], kern_v[1, w, pl.ds(j, chunk)]], 1)
                acc[h, w, :] += dot(lhs, rhs, ((1,), (0,)))

        j_last, rhs_last = get_rhs(nch - 1)

        def last(row):
            w = pl.ds(pl.multiple_of(row, rows), rows)
            lhs = jnp.concatenate(
                [kern_v[0, w, pl.ds(j_last, chunk)], kern_v[1, w, pl.ds(j_last, chunk)]], 1)
            return acc[h, w, :] + dot(lhs, rhs_last, ((1,), (0,)))

        @pl.loop(1, nf + 1)
        def _(e):
            d = lax.rem(e, nf)
            part_s[h, d] = last((1 - core) * half + dest_of(d) * rows).astype(BF)
            cp(d, h).start()

        @pl.loop(1, nf + 1)
        def _(e):
            d = lax.rem(e, nf)
            own = last(core * half + dest_of(d) * rows)
            cp(d, h).wait_recv()
            g_s[h, dest_of(d)] = (own + part_r[h, d].astype(F32)).astype(BF)

            @pl.when(d != 0)
            def _():
                c2(d, h).start()

    def window(h):
        g_f[me] = g_s[h, me].astype(F32)

        @pl.loop(1, nf)
        def _(d):
            c2(d, h).wait_recv()
            g_f[src_of(d)] = g_r[h, src_of(d)].astype(F32)

        @pl.loop(1, nf + 1)
        def _(e):
            d = lax.rem(e, nf)
            a = dest_of(d)

            @pl.loop(0, rows // 16)
            def _(t):
                w = pl.ds(pl.multiple_of(t * 16, 16), 16)
                total = jnp.zeros((16, np_), F32)
                for f in range(nf):
                    total = total + (dk[h, a - f + nf - 1, w, :] + dk[h, a + f + nd, w, :]) * g_f[f, w, :]
                m_s[h, a, w, :] = total.astype(BF)

            @pl.when(d != 0)
            def _():
                c3(d, h).start()

        m_r[h, me] = m_s[h, me]

    def adjoint_product(h):
        def add(buf, owner, src):
            m = buf[h, src]
            lhs = jnp.concatenate([m, swap(m, False)], 0)
            w = pl.ds(pl.multiple_of(owner * half + src * rows, rows), rows)
            rhs = jnp.concatenate([kern_v[0, w, :], kern_v[1, w, :]], 0)
            acc2[h] += dot(lhs, rhs, ((0,), (0,)))

        @pl.loop(0, nf)
        def _(d):
            @pl.when(d != 0)
            def _():
                c3(d, h).wait_recv()

            co(d, h).start()
            add(m_r, core, src_of(d))

            @pl.when(d != 0)
            def _():
                co(d - 1, h).wait_recv()
                add(m_o, 1 - core, src_of(d - 1))

        co(nf - 1, h).wait_recv()
        add(m_o, 1 - core, src_of(nf - 1))

        @pl.loop(1, nch + 1)
        def _(e):
            q = lax.rem(q0 - e + 2 * nch, nch)
            w = pl.ds(pl.multiple_of(q * chunk, chunk), chunk)
            t = jnp.swapaxes(acc2[h, :, w], 0, 1).astype(BF)
            h_s[h, pl.ds(q * per, per)] = t.reshape(per, rows, np_)

            @pl.loop(0, per)
            def _(j):
                d = lax.rem(me - (q * per + j) + nf, nf)

                @pl.when(d != 0)
                def _():
                    c4(d, h).start()

    for stage in (forward_product, window, adjoint_product):
        for h in range(2):
            stage(h)

    keep = [pltpu.make_async_copy(h_s.at[h, me], out_hbm.at[h, me], load_sem.at[h]) for h in range(2)]
    for h in range(2):
        keep[h].start()

    @pl.loop(1, nf)
    def _(d):
        for b in range(NSUB):
            c1(d, 0, b).wait_send()
        c1(d, 1, 0).wait_send()
        for h in range(2):
            c2(d, h).wait_send()
            c3(d, h).wait_send()
            c4(d, h).wait_send()

    @pl.loop(0, nf)
    def _(d):
        for h in range(2):
            cp(d, h).wait_send()
            co(d, h).wait_send()

    @pl.loop(1, nf)
    def _(d):
        for h in range(2):
            c4(d, h).wait_recv()

    okeep.wait()
    for h in range(2):
        keep[h].wait()


def final_kernel(nf, step_rows, width, np_, nt, h_ref, ons_ref, foc_ref, tab_ref, out_ref, rows_f):
    nk = 2 * nf
    ph = np_ // 2
    tied = 128 // width
    for f in range(nf):
        a, b = h_ref[0, f].astype(F32), h_ref[1, f].astype(F32)
        rows_f[pl.ds(f, step_rows, stride=width), :] = jnp.concatenate([a[:, :ph], b[:, :ph]], 1)
        rows_f[pl.ds(nf + f, step_rows, stride=width), :] = jnp.concatenate([a[:, ph:], b[:, ph:]], 1)
    rows_f[pl.ds(nk, step_rows, stride=width), :] = ons_ref[...].astype(F32)

    @pl.when(pl.program_id(0) == 0)
    def _():
        for k in range(nk + 1, width):
            rows_f[pl.ds(k, step_rows, stride=width), :] = jnp.full(
                (step_rows, np_), 1.0 if k == nk + 1 else 0.0, F32)

    groups = step_rows // tied
    cols = []
    for g in range(groups):
        t = jnp.swapaxes(rows_f[pl.ds(g * 128, 128), :], 0, 1).astype(BF)
        cols.append(jnp.concatenate([t, t], 1))
    for i in range(tied):
        for g in range(groups):
            x = g * tied + i
            both = dot(cols[g], tab_ref[i], ((1,), (0,)))
            f = foc_ref[x].astype(F32)
            out_ref[x] = (f + jnp.where(both[:, nt:] > 0.0, both[:, :nt], 0.0)).astype(BF)


def shards(kernel, focus, onset):
    nf = lax.axis_size("freq")
    rows, np_, nt = focus.shape
    half = nf * rows
    table = forward_table(nt, nf)
    nk = 2 * nf
    table = table.reshape(nf, 2, nt).swapaxes(0, 1).reshape(nk, nt)
    fwd = jnp.asarray(np.concatenate(split(table), 0))
    inv_hi, inv_lo = split((table * np.float32(2.0 / nt)).astype(np.float32))
    t = np.arange(nt)
    width = 32
    while width < nk + 2:
        width *= 2
    tied = 128 // width
    right = np.zeros((tied, 256, 2 * nt), np.float32).astype(jnp.bfloat16)
    for i in range(tied):
        at = i * width
        right[i, at:at + nk, :nt] = inv_hi
        right[i, 128 + at:128 + at + nk, :nt] = inv_lo
        right[i, at + nk, nt:] = 1.0
        right[i, at + nk + 1, nt:] = -np.minimum(t, nt - t)
    right = jnp.asarray(right)

    def vm(shape, kind=BF):
        return pltpu.VMEM(shape, kind)

    one = (nf, rows, np_)
    block = (2,) + one
    dma = pltpu.SemaphoreType.DMA
    spectra, own = pl.pallas_call(
        functools.partial(spectra_kernel, nf, rows, np_, nt),
        out_shape=[jax.ShapeDtypeStruct(block, BF), jax.ShapeDtypeStruct((rows, np_), jnp.int32)],
        in_specs=[pl.BlockSpec(memory_space=pl.ANY)] * 3 + [pl.BlockSpec(memory_space=pltpu.VMEM)],
        out_specs=[pl.BlockSpec(memory_space=pl.ANY)] * 2,
        scratch_shapes=[
            vm((2, 2 * half, half)), vm((rows, np_, nt)), vm((rows, np_), jnp.int32),
            vm((2, rows * nf, np_), F32),
            vm(block), vm(block), vm((2, 2 * half, np_), F32),
            vm(block), vm(block),
            vm(block), vm(block), vm(one, F32), vm((2, 4 * nf - 2, rows, np_), F32),
            vm(block), vm(block), vm(block), vm((2, np_, half), F32), vm(block),
            dma((NSUB + 2,)), dma((NSUB + 1, nf)), dma((NSUB + 1, nf)),
        ] + [dma((2, nf))] * 10,
        compiler_params=pltpu.CompilerParams(
            collective_id=0, has_side_effects=True, vmem_limit_bytes=58 << 20),
        cost_estimate=pl.CostEstimate(
            flops=32 * half * half * np_, bytes_accessed=8 * half * half, transcendentals=0),
    )(kernel, focus, onset, fwd)
    sr = 16
    return pl.pallas_call(
        functools.partial(final_kernel, nf, sr, width, np_, nt),
        out_shape=jax.ShapeDtypeStruct(focus.shape, BF),
        grid=(rows // sr,),
        in_specs=[
            pl.BlockSpec((2, nf, sr, np_), lambda i: (0, 0, i, 0)),
            pl.BlockSpec((sr, np_), lambda i: (i, 0)),
            pl.BlockSpec((sr, np_, nt), lambda i: (i, 0, 0)),
            pl.BlockSpec(right.shape, lambda i: (0, 0, 0)),
        ],
        out_specs=pl.BlockSpec((sr, np_, nt), lambda i: (i, 0, 0)),
        scratch_shapes=[pltpu.VMEM((sr * width, np_), F32)],
        compiler_params=pltpu.CompilerParams(vmem_limit_bytes=58 << 20),
    )(spectra, own, focus, right)


def solution(mesh):
    in_specs = (P("freq", None, None, "rcv"), P(("rcv", "freq"), "grp", None), P(None, "grp"))
    out_specs = P(("rcv", "freq"), "grp", None)
    return jax.shard_map(shards, mesh=mesh, in_specs=in_specs, out_specs=out_specs, check_vma=False)
```

```python
import functools
import math

import jax
import jax.numpy as jnp
import numpy as np
from jax import lax
from jax.experimental import pallas as pl
from jax.experimental.pallas import tpu as pltpu
from jax.sharding import PartitionSpec as P

MESH = pl.DeviceIdType.MESH
NSUB = 2
BF = jnp.bfloat16
F32 = jnp.float32


def forward_table(nt, nf):
    phase = ((np.arange(1, nf + 1)[:, None] * np.arange(nt)[None, :]) % nt) * (2.0 * math.pi / nt)
    return np.stack([np.cos(phase), -np.sin(phase)], axis=1).reshape(2 * nf, nt).astype(np.float32)


def split(table):
    high = table.astype(jnp.bfloat16)
    low = (table - high.astype(np.float32)).astype(jnp.bfloat16)
    return high, low


def dot(a, b, dims):
    return lax.dot_general(a, b, (dims, ((), ())), preferred_element_type=F32)


def swap(block, first):
    h = block.shape[1] // 2
    re, im = block[:, :h], block[:, h:]
    return jnp.concatenate([-im, re] if first else [im, -re], 1)


def spectra_kernel(
    nf, rows, np_, nt, kern_hbm, foc_hbm, ons_hbm, tab_ref, out_hbm, ons_out,
    kern_v, foc_v, ons_v, spec_f, spec_s, spec_r, acc, part_s, part_r, g_s, g_r, g_f, dk,
    m_s, m_r, m_o, acc2, h_s,
    load_sem, s1, r1, sp, rp, s2, r2, s3, r3, so, ro, s4, r4,
):
    me = lax.axis_index("freq")
    core = lax.axis_index("rcv")
    nk = 2 * nf
    ph = np_ // 2
    half = nf * rows
    sub = rows // NSUB
    per = max(1, 128 // rows)
    chunk = per * rows
    nch = half // chunk
    nd = 2 * nf - 1

    def dest_of(d):
        return lax.rem(me - d + nf, nf)

    def src_of(d):
        return lax.rem(me + d, nf)

    def peer(src, dst, ssem, rsem, dest):
        return pltpu.make_async_remote_copy(
            src_ref=src, dst_ref=dst, send_sem=ssem, recv_sem=rsem,
            device_id={"freq": dest}, device_id_type=MESH)

    def mate(src, dst, ssem, rsem):
        return pltpu.make_async_remote_copy(
            src_ref=src, dst_ref=dst, send_sem=ssem, recv_sem=rsem,
            device_id={"rcv": 1 - core}, device_id_type=MESH)

    def c1(d, h, b):
        w = pl.ds(b * sub, sub) if h == 0 else pl.ds(0, rows)
        i = b if h == 0 else NSUB
        return peer(spec_s.at[h, dest_of(d), w], spec_r.at[h, me, w], s1.at[i, d], r1.at[i, d], dest_of(d))

    def cp(d, h):
        return mate(part_s.at[h, d], part_r.at[h, d], sp.at[h, d], rp.at[h, d])

    def c2(d, h):
        return peer(g_s.at[h, dest_of(d)], g_r.at[h, me], s2.at[h, d], r2.at[h, d], dest_of(d))

    def c3(d, h):
        return peer(m_s.at[h, dest_of(d)], m_r.at[h, me], s3.at[h, d], r3.at[h, d], dest_of(d))

    def co(d, h):
        return mate(m_r.at[h, src_of(d)], m_o.at[h, src_of(d)], so.at[h, d], ro.at[h, d])

    def c4(d, h):
        return peer(h_s.at[h, dest_of(d)], out_hbm.at[h, me], s4.at[h, d], r4.at[h, d], dest_of(d))

    loads = [pltpu.make_async_copy(foc_hbm.at[pl.ds(b * sub, sub)], foc_v.at[pl.ds(b * sub, sub)], load_sem.at[b])
             for b in range(NSUB)]
    kload = pltpu.make_async_copy(kern_hbm.at[0], kern_v, load_sem.at[NSUB])
    oload = pltpu.make_async_copy(
        ons_hbm.at[pl.ds(pl.multiple_of((core * nf + me) * rows, rows), rows)], ons_v, load_sem.at[NSUB + 1])
    for load in loads:
        load.start()
    oload.start()
    kload.start()

    barrier = pltpu.get_barrier_semaphore()

    @pl.loop(1, nf)
    def _(d):
        pl.semaphore_signal(barrier, inc=1, device_id={"freq": dest_of(d)}, device_id_type=MESH)

    pl.semaphore_signal(barrier, inc=1, device_id={"rcv": 1 - core}, device_id_type=MESH)

    for b in range(NSUB):
        loads[b].wait()

        @pl.loop(0, sub // 2, unroll=4)
        def _(i):
            x = b * sub + 2 * i
            f = foc_v[pl.ds(x, 2)].reshape(2 * np_, nt)
            s = dot(tab_ref[...], f, ((1,), (1,)))
            s = s[:nk] + s[nk:]
            for y in range(2):
                for h in range(2):
                    lo = y * np_ + h * ph
                    spec_f[h, pl.ds((x + y) * nf, nf), :] = jnp.concatenate(
                        [s[:nf, lo:lo + ph], s[nf:, lo:lo + ph]], 1)

        for h in range(2):
            for k in range(nf):
                v = spec_f[h, pl.ds(b * sub * nf + k, sub, stride=nf), :]
                spec_s[h, k, pl.ds(b * sub, sub), :] = v.astype(BF)
            if h == 0:
                if b == 0:
                    pl.semaphore_wait(barrier, nf)

                @pl.loop(1, nf)
                def _(d):
                    c1(d, 0, b).start()

    @pl.loop(1, nf)
    def _(d):
        c1(d, 1, 0).start()

    for h in range(2):
        spec_r[h, me] = spec_s[h, me]

    oload.wait()
    okeep = pltpu.make_async_copy(ons_v, ons_out, load_sem.at[NSUB + 1])
    okeep.start()
    real = lax.broadcasted_iota(jnp.int32, (rows, np_), 1) < ph
    for h in range(2):
        on = ons_v[:, h * ph:(h + 1) * ph].astype(F32)
        on = jnp.concatenate([on, on], 1)
        theta = (on - 0.5) * (2.0 * math.pi / nt)
        c_1, s_1 = jnp.cos(theta), jnp.sin(theta)
        dk[h, nf - 1] = (2.0 * on - 1.0) * (1.0 / nt)
        cm, sm = c_1, s_1
        for m in range(1, 2 * nf + 1):
            value = sm * (1.0 / (nt * math.sin(math.pi * m / nt)))
            if m < nf:
                dk[h, nf - 1 + m] = value
                dk[h, nf - 1 - m] = value
            if m > 1:
                dk[h, nd + m - 2] = jnp.where(real, value, -value)
            cm, sm = cm * c_1 - sm * s_1, sm * c_1 + cm * s_1

    acc[...] = jnp.zeros_like(acc)
    acc2[...] = jnp.zeros_like(acc2)
    kload.wait()

    q0 = me // per
    tile = half

    def forward_product(h):
        def get_rhs(step):
            q = lax.rem(q0 + step, nch)

            @pl.loop(0, per)
            def _(j):
                d = lax.rem(q * per + j - me + nf, nf)

                @pl.when(d != 0)
                def _():
                    for b in range(NSUB if h == 0 else 1):
                        c1(d, h, b).wait_recv()

            s = spec_r[h, pl.ds(q * per, per)].reshape(chunk, np_)
            return pl.multiple_of(q * chunk, chunk), jnp.concatenate([s, swap(s, True)], 0)

        @pl.loop(0, nch - 1)
        def _(step):
            j, rhs = get_rhs(step)

            @pl.loop(0, 2 * half // tile)
            def _(t):
                w = pl.ds(pl.multiple_of(t * tile, tile), tile)
                lhs = jnp.concatenate([kern_v[0, w, pl.ds(j, chunk)], kern_v[1, w, pl.ds(j, chunk)]], 1)
                acc[h, w, :] += dot(lhs, rhs, ((1,), (0,)))

        j_last, rhs_last = get_rhs(nch - 1)

        def last(row):
            w = pl.ds(pl.multiple_of(row, rows), rows)
            lhs = jnp.concatenate(
                [kern_v[0, w, pl.ds(j_last, chunk)], kern_v[1, w, pl.ds(j_last, chunk)]], 1)
            return acc[h, w, :] + dot(lhs, rhs_last, ((1,), (0,)))

        @pl.loop(1, nf + 1)
        def _(e):
            d = lax.rem(e, nf)
            part_s[h, d] = last((1 - core) * half + dest_of(d) * rows).astype(BF)
            cp(d, h).start()

        @pl.loop(1, nf + 1)
        def _(e):
            d = lax.rem(e, nf)
            own = last(core * half + dest_of(d) * rows)
            cp(d, h).wait_recv()
            g_s[h, dest_of(d)] = (own + part_r[h, d].astype(F32)).astype(BF)

            @pl.when(d != 0)
            def _():
                c2(d, h).start()

    def window(h):
        g_f[me] = g_s[h, me].astype(F32)

        @pl.loop(1, nf)
        def _(d):
            c2(d, h).wait_recv()
            g_f[src_of(d)] = g_r[h, src_of(d)].astype(F32)

        @pl.loop(1, nf + 1)
        def _(e):
            d = lax.rem(e, nf)
            a = dest_of(d)

            @pl.loop(0, rows // 16)
            def _(t):
                w = pl.ds(pl.multiple_of(t * 16, 16), 16)
                total = jnp.zeros((16, np_), F32)
                for f in range(nf):
                    total = total + (dk[h, a - f + nf - 1, w, :] + dk[h, a + f + nd, w, :]) * g_f[f, w, :]
                m_s[h, a, w, :] = total.astype(BF)

            @pl.when(d != 0)
            def _():
                c3(d, h).start()

        m_r[h, me] = m_s[h, me]

    def adjoint_product(h):
        def add(buf, owner, src):
            m = buf[h, src]
            lhs = jnp.concatenate([m, swap(m, False)], 0)
            w = pl.ds(pl.multiple_of(owner * half + src * rows, rows), rows)
            rhs = jnp.concatenate([kern_v[0, w, :], kern_v[1, w, :]], 0)
            acc2[h] += dot(lhs, rhs, ((0,), (0,)))

        @pl.loop(0, nf)
        def _(d):
            @pl.when(d != 0)
            def _():
                c3(d, h).wait_recv()

            co(d, h).start()
            add(m_r, core, src_of(d))

            @pl.when(d != 0)
            def _():
                co(d - 1, h).wait_recv()
                add(m_o, 1 - core, src_of(d - 1))

        co(nf - 1, h).wait_recv()
        add(m_o, 1 - core, src_of(nf - 1))

        @pl.loop(1, nch + 1)
        def _(e):
            q = lax.rem(q0 - e + 2 * nch, nch)
            w = pl.ds(pl.multiple_of(q * chunk, chunk), chunk)
            t = jnp.swapaxes(acc2[h, :, w], 0, 1).astype(BF)
            h_s[h, pl.ds(q * per, per)] = t.reshape(per, rows, np_)

            @pl.loop(0, per)
            def _(j):
                d = lax.rem(me - (q * per + j) + nf, nf)

                @pl.when(d != 0)
                def _():
                    c4(d, h).start()

    for stage in (forward_product, window, adjoint_product):
        for h in range(2):
            stage(h)

    keep = [pltpu.make_async_copy(h_s.at[h, me], out_hbm.at[h, me], load_sem.at[h]) for h in range(2)]
    for h in range(2):
        keep[h].start()

    @pl.loop(1, nf)
    def _(d):
        for b in range(NSUB):
            c1(d, 0, b).wait_send()
        c1(d, 1, 0).wait_send()
        for h in range(2):
            c2(d, h).wait_send()
            c3(d, h).wait_send()
            c4(d, h).wait_send()

    @pl.loop(0, nf)
    def _(d):
        for h in range(2):
            cp(d, h).wait_send()
            co(d, h).wait_send()

    @pl.loop(1, nf)
    def _(d):
        for h in range(2):
            c4(d, h).wait_recv()

    okeep.wait()
    for h in range(2):
        keep[h].wait()


def final_kernel(nf, step_rows, width, np_, nt, h_ref, ons_ref, foc_ref, tab_ref, out_ref, rows_f):
    nk = 2 * nf
    ph = np_ // 2
    tied = 128 // width
    for f in range(nf):
        a, b = h_ref[0, f].astype(F32), h_ref[1, f].astype(F32)
        rows_f[pl.ds(f, step_rows, stride=width), :] = jnp.concatenate([a[:, :ph], b[:, :ph]], 1)
        rows_f[pl.ds(nf + f, step_rows, stride=width), :] = jnp.concatenate([a[:, ph:], b[:, ph:]], 1)
    rows_f[pl.ds(nk, step_rows, stride=width), :] = ons_ref[...].astype(F32)

    @pl.when(pl.program_id(0) == 0)
    def _():
        for k in range(nk + 1, width):
            rows_f[pl.ds(k, step_rows, stride=width), :] = jnp.zeros((step_rows, np_), F32)

    groups = step_rows // tied
    sample = lax.broadcasted_iota(jnp.int32, (np_, nt), 1)
    edge = jnp.minimum(sample, nt - sample).astype(F32)
    for g in range(groups):
        t = jnp.swapaxes(rows_f[pl.ds(g * 128, 128), :], 0, 1)
        col = t.astype(BF)
        for i in range(tied):
            x = g * tied + i
            update = dot(jnp.concatenate([col, col], 1), tab_ref[i], ((1,), (0,)))
            limit = t[:, i * width + nk:i * width + nk + 1]
            f = foc_ref[x].astype(F32)
            out_ref[x] = (f + jnp.where(edge < limit, update, 0.0)).astype(BF)


def shards(kernel, focus, onset):
    nf = lax.axis_size("freq")
    rows, np_, nt = focus.shape
    half = nf * rows
    table = forward_table(nt, nf)
    nk = 2 * nf
    table = table.reshape(nf, 2, nt).swapaxes(0, 1).reshape(nk, nt)
    fwd = jnp.asarray(np.concatenate(split(table), 0))
    inv_hi, inv_lo = split((table * np.float32(2.0 / nt)).astype(np.float32))
    width = 32
    while width < nk + 2:
        width *= 2
    tied = 128 // width
    right = np.zeros((tied, 256, nt), np.float32).astype(jnp.bfloat16)
    for i in range(tied):
        at = i * width
        right[i, at:at + nk] = inv_hi
        right[i, 128 + at:128 + at + nk] = inv_lo
    right = jnp.asarray(right)

    def vm(shape, kind=BF):
        return pltpu.VMEM(shape, kind)

    one = (nf, rows, np_)
    block = (2,) + one
    dma = pltpu.SemaphoreType.DMA
    spectra, own = pl.pallas_call(
        functools.partial(spectra_kernel, nf, rows, np_, nt),
        out_shape=[jax.ShapeDtypeStruct(block, BF), jax.ShapeDtypeStruct((rows, np_), jnp.int32)],
        in_specs=[pl.BlockSpec(memory_space=pl.ANY)] * 3 + [pl.BlockSpec(memory_space=pltpu.VMEM)],
        out_specs=[pl.BlockSpec(memory_space=pl.ANY)] * 2,
        scratch_shapes=[
            vm((2, 2 * half, half)), vm((rows, np_, nt)), vm((rows, np_), jnp.int32),
            vm((2, rows * nf, np_), F32),
            vm(block), vm(block), vm((2, 2 * half, np_), F32),
            vm(block), vm(block),
            vm(block), vm(block), vm(one, F32), vm((2, 4 * nf - 2, rows, np_), F32),
            vm(block), vm(block), vm(block), vm((2, np_, half), F32), vm(block),
            dma((NSUB + 2,)), dma((NSUB + 1, nf)), dma((NSUB + 1, nf)),
        ] + [dma((2, nf))] * 10,
        compiler_params=pltpu.CompilerParams(
            collective_id=0, has_side_effects=True, vmem_limit_bytes=58 << 20),
        cost_estimate=pl.CostEstimate(
            flops=32 * half * half * np_, bytes_accessed=8 * half * half, transcendentals=0),
    )(kernel, focus, onset, fwd)
    sr = min(rows, 32)
    return pl.pallas_call(
        functools.partial(final_kernel, nf, sr, width, np_, nt),
        out_shape=jax.ShapeDtypeStruct(focus.shape, BF),
        grid=(rows // sr,),
        in_specs=[
            pl.BlockSpec((2, nf, sr, np_), lambda i: (0, 0, i, 0)),
            pl.BlockSpec((sr, np_), lambda i: (i, 0)),
            pl.BlockSpec((sr, np_, nt), lambda i: (i, 0, 0)),
            pl.BlockSpec(right.shape, lambda i: (0, 0, 0)),
        ],
        out_specs=pl.BlockSpec((sr, np_, nt), lambda i: (i, 0, 0)),
        scratch_shapes=[pltpu.VMEM((sr * width, np_), F32)],
        compiler_params=pltpu.CompilerParams(vmem_limit_bytes=58 << 20),
    )(spectra, own, focus, right)


def solution(mesh):
    in_specs = (P("freq", None, None, "rcv"), P(("rcv", "freq"), "grp", None), P(None, "grp"))
    out_specs = P(("rcv", "freq"), "grp", None)
    return jax.shard_map(shards, mesh=mesh, in_specs=in_specs, out_specs=out_specs, check_vma=False)
```

```python
import functools
import math

import jax
import jax.numpy as jnp
import numpy as np
from jax import lax
from jax.experimental import pallas as pl
from jax.experimental.pallas import tpu as pltpu
from jax.sharding import PartitionSpec as P

MESH = pl.DeviceIdType.MESH
NSUB = 2
BF = jnp.bfloat16
F32 = jnp.float32


def forward_table(nt, nf):
    phase = ((np.arange(1, nf + 1)[:, None] * np.arange(nt)[None, :]) % nt) * (2.0 * math.pi / nt)
    return np.stack([np.cos(phase), -np.sin(phase)], axis=1).reshape(2 * nf, nt).astype(np.float32)


def split(table):
    high = table.astype(jnp.bfloat16)
    low = (table - high.astype(np.float32)).astype(jnp.bfloat16)
    return high, low


def dot(a, b, dims):
    return lax.dot_general(a, b, (dims, ((), ())), preferred_element_type=F32)


def swap(block, first):
    h = block.shape[1] // 2
    re, im = block[:, :h], block[:, h:]
    return jnp.concatenate([-im, re] if first else [im, -re], 1)


def spectra_kernel(
    nf, rows, np_, nt, kern_hbm, foc_hbm, ons_hbm, tab_ref, out_hbm, ons_out,
    kern_v, foc_v, ons_v, spec_f, spec_s, spec_r, acc, part_s, part_r, g_s, g_r, g_f, dk,
    m_s, m_r, m_o, acc2, h_s,
    load_sem, s1, r1, sp, rp, s2, r2, s3, r3, so, ro, s4, r4,
):
    me = lax.axis_index("freq")
    core = lax.axis_index("rcv")
    nk = 2 * nf
    ph = np_ // 2
    half = nf * rows
    sub = rows // NSUB
    per = max(1, 128 // rows)
    chunk = per * rows
    nch = half // chunk
    nd = 2 * nf - 1

    def dest_of(d):
        return lax.rem(me - d + nf, nf)

    def src_of(d):
        return lax.rem(me + d, nf)

    def peer(src, dst, ssem, rsem, dest):
        return pltpu.make_async_remote_copy(
            src_ref=src, dst_ref=dst, send_sem=ssem, recv_sem=rsem,
            device_id={"freq": dest}, device_id_type=MESH)

    def mate(src, dst, ssem, rsem):
        return pltpu.make_async_remote_copy(
            src_ref=src, dst_ref=dst, send_sem=ssem, recv_sem=rsem,
            device_id={"rcv": 1 - core}, device_id_type=MESH)

    def c1(d, h, b):
        w = pl.ds(b * sub, sub) if h == 0 else pl.ds(0, rows)
        i = b if h == 0 else NSUB
        return peer(spec_s.at[h, dest_of(d), w], spec_r.at[h, me, w], s1.at[i, d], r1.at[i, d], dest_of(d))

    def cp(d, h):
        return mate(part_s.at[h, d], part_r.at[h, d], sp.at[h, d], rp.at[h, d])

    def c2(d, h):
        return peer(g_s.at[h, dest_of(d)], g_r.at[h, me], s2.at[h, d], r2.at[h, d], dest_of(d))

    def c3(d, h):
        return peer(m_s.at[h, dest_of(d)], m_r.at[h, me], s3.at[h, d], r3.at[h, d], dest_of(d))

    def co(d, h):
        return mate(m_r.at[h, src_of(d)], m_o.at[h, src_of(d)], so.at[h, d], ro.at[h, d])

    def c4(d, h):
        return peer(h_s.at[h, dest_of(d)], out_hbm.at[h, me], s4.at[h, d], r4.at[h, d], dest_of(d))

    loads = [pltpu.make_async_copy(foc_hbm.at[pl.ds(b * sub, sub)], foc_v.at[pl.ds(b * sub, sub)], load_sem.at[b])
             for b in range(NSUB)]
    kload = pltpu.make_async_copy(kern_hbm.at[0], kern_v, load_sem.at[NSUB])
    oload = pltpu.make_async_copy(
        ons_hbm.at[pl.ds(pl.multiple_of((core * nf + me) * rows, rows), rows)], ons_v, load_sem.at[NSUB + 1])
    for load in loads:
        load.start()
    oload.start()
    kload.start()

    barrier = pltpu.get_barrier_semaphore()

    @pl.loop(1, nf)
    def _(d):
        pl.semaphore_signal(barrier, inc=1, device_id={"freq": dest_of(d)}, device_id_type=MESH)

    pl.semaphore_signal(barrier, inc=1, device_id={"rcv": 1 - core}, device_id_type=MESH)

    for b in range(NSUB):
        loads[b].wait()

        @pl.loop(0, sub // 2, unroll=4)
        def _(i):
            x = b * sub + 2 * i
            f = foc_v[pl.ds(x, 2)].reshape(2 * np_, nt)
            s = dot(tab_ref[...], f, ((1,), (1,)))
            s = s[:nk] + s[nk:]
            for y in range(2):
                for h in range(2):
                    lo = y * np_ + h * ph
                    spec_f[h, pl.ds((x + y) * nf, nf), :] = jnp.concatenate(
                        [s[:nf, lo:lo + ph], s[nf:, lo:lo + ph]], 1)

        for h in range(2):
            for k in range(nf):
                v = spec_f[h, pl.ds(b * sub * nf + k, sub, stride=nf), :]
                spec_s[h, k, pl.ds(b * sub, sub), :] = v.astype(BF)
            if h == 0:
                if b == 0:
                    pl.semaphore_wait(barrier, nf)

                @pl.loop(1, nf)
                def _(d):
                    c1(d, 0, b).start()

    @pl.loop(1, nf)
    def _(d):
        c1(d, 1, 0).start()

    for h in range(2):
        spec_r[h, me] = spec_s[h, me]

    oload.wait()
    okeep = pltpu.make_async_copy(ons_v, ons_out, load_sem.at[NSUB + 1])
    okeep.start()
    real = lax.broadcasted_iota(jnp.int32, (rows, np_), 1) < ph
    for h in range(2):
        on = ons_v[:, h * ph:(h + 1) * ph].astype(F32)
        on = jnp.concatenate([on, on], 1)
        theta = (on - 0.5) * (2.0 * math.pi / nt)
        c_1, s_1 = jnp.cos(theta), jnp.sin(theta)
        dk[h, nf - 1] = (2.0 * on - 1.0) * (1.0 / nt)
        cm, sm = c_1, s_1
        for m in range(1, 2 * nf + 1):
            value = sm * (1.0 / (nt * math.sin(math.pi * m / nt)))
            if m < nf:
                dk[h, nf - 1 + m] = value
                dk[h, nf - 1 - m] = value
            if m > 1:
                dk[h, nd + m - 2] = jnp.where(real, value, -value)
            cm, sm = cm * c_1 - sm * s_1, sm * c_1 + cm * s_1

    acc[...] = jnp.zeros_like(acc)
    acc2[...] = jnp.zeros_like(acc2)
    kload.wait()

    q0 = me // per
    tile = half

    def forward_product(h):
        def get_rhs(step):
            q = lax.rem(q0 + step, nch)

            @pl.loop(0, per)
            def _(j):
                d = lax.rem(q * per + j - me + nf, nf)

                @pl.when(d != 0)
                def _():
                    for b in range(NSUB if h == 0 else 1):
                        c1(d, h, b).wait_recv()

            s = spec_r[h, pl.ds(q * per, per)].reshape(chunk, np_)
            return pl.multiple_of(q * chunk, chunk), jnp.concatenate([s, swap(s, True)], 0)

        @pl.loop(0, nch - 1)
        def _(step):
            j, rhs = get_rhs(step)

            @pl.loop(0, 2 * half // tile)
            def _(t):
                w = pl.ds(pl.multiple_of(t * tile, tile), tile)
                lhs = jnp.concatenate([kern_v[0, w, pl.ds(j, chunk)], kern_v[1, w, pl.ds(j, chunk)]], 1)
                acc[h, w, :] += dot(lhs, rhs, ((1,), (0,)))

        j_last, rhs_last = get_rhs(nch - 1)

        def last(owner):
            w = pl.ds(pl.multiple_of(owner * half, half), half)
            lhs = jnp.concatenate(
                [kern_v[0, w, pl.ds(j_last, chunk)], kern_v[1, w, pl.ds(j_last, chunk)]], 1)
            acc[h, w, :] += dot(lhs, rhs_last, ((1,), (0,)))

        def block(owner, d):
            return acc[h, pl.ds(pl.multiple_of(owner * half + dest_of(d) * rows, rows), rows), :]

        last(1 - core)

        @pl.loop(1, nf + 1)
        def _(e):
            d = lax.rem(e, nf)
            part_s[h, d] = block(1 - core, d).astype(BF)
            cp(d, h).start()

        last(core)

        @pl.loop(1, nf + 1)
        def _(e):
            d = lax.rem(e, nf)
            cp(d, h).wait_recv()
            g_s[h, dest_of(d)] = (block(core, d) + part_r[h, d].astype(F32)).astype(BF)

            @pl.when(d != 0)
            def _():
                c2(d, h).start()

    def window(h):
        g_f[me] = g_s[h, me].astype(F32)

        @pl.loop(1, nf)
        def _(d):
            c2(d, h).wait_recv()
            g_f[src_of(d)] = g_r[h, src_of(d)].astype(F32)

        @pl.loop(1, nf + 1)
        def _(e):
            d = lax.rem(e, nf)
            a = dest_of(d)

            @pl.loop(0, rows // 16)
            def _(t):
                w = pl.ds(pl.multiple_of(t * 16, 16), 16)
                total = jnp.zeros((16, np_), F32)
                for f in range(nf):
                    total = total + (dk[h, a - f + nf - 1, w, :] + dk[h, a + f + nd, w, :]) * g_f[f, w, :]
                m_s[h, a, w, :] = total.astype(BF)

            @pl.when(d != 0)
            def _():
                c3(d, h).start()

        m_r[h, me] = m_s[h, me]

    def adjoint_product(h):
        def add(*terms):
            lhs, rhs = [], []
            for buf, owner, src in terms:
                m = buf[h, src]
                w = pl.ds(pl.multiple_of(owner * half + src * rows, rows), rows)
                lhs += [m, swap(m, False)]
                rhs += [kern_v[0, w, :], kern_v[1, w, :]]
            acc2[h] += dot(jnp.concatenate(lhs, 0), jnp.concatenate(rhs, 0), ((0,), (0,)))

        co(0, h).start()
        add((m_r, core, me))

        @pl.loop(1, nf)
        def _(d):
            c3(d, h).wait_recv()
            co(d, h).start()
            co(d - 1, h).wait_recv()
            add((m_r, core, src_of(d)), (m_o, 1 - core, src_of(d - 1)))

        co(nf - 1, h).wait_recv()
        add((m_o, 1 - core, src_of(nf - 1)))

        @pl.loop(1, nch + 1)
        def _(e):
            q = lax.rem(q0 - e + 2 * nch, nch)
            w = pl.ds(pl.multiple_of(q * chunk, chunk), chunk)
            t = jnp.swapaxes(acc2[h, :, w], 0, 1).astype(BF)
            h_s[h, pl.ds(q * per, per)] = t.reshape(per, rows, np_)

            @pl.loop(0, per)
            def _(j):
                d = lax.rem(me - (q * per + j) + nf, nf)

                @pl.when(d != 0)
                def _():
                    c4(d, h).start()

    for stage in (forward_product, window, adjoint_product):
        for h in range(2):
            stage(h)

    keep = [pltpu.make_async_copy(h_s.at[h, me], out_hbm.at[h, me], load_sem.at[h]) for h in range(2)]
    for h in range(2):
        keep[h].start()

    @pl.loop(1, nf)
    def _(d):
        for b in range(NSUB):
            c1(d, 0, b).wait_send()
        c1(d, 1, 0).wait_send()
        for h in range(2):
            c2(d, h).wait_send()
            c3(d, h).wait_send()
            c4(d, h).wait_send()

    @pl.loop(0, nf)
    def _(d):
        for h in range(2):
            cp(d, h).wait_send()
            co(d, h).wait_send()

    @pl.loop(1, nf)
    def _(d):
        for h in range(2):
            c4(d, h).wait_recv()

    okeep.wait()
    for h in range(2):
        keep[h].wait()


def final_kernel(nf, step_rows, width, np_, nt, h_ref, ons_ref, foc_ref, tab_ref, out_ref, rows_f):
    nk = 2 * nf
    ph = np_ // 2
    tied = 128 // width
    for f in range(nf):
        a, b = h_ref[0, f].astype(F32), h_ref[1, f].astype(F32)
        rows_f[pl.ds(f, step_rows, stride=width), :] = jnp.concatenate([a[:, :ph], b[:, :ph]], 1)
        rows_f[pl.ds(nf + f, step_rows, stride=width), :] = jnp.concatenate([a[:, ph:], b[:, ph:]], 1)
    rows_f[pl.ds(nk, step_rows, stride=width), :] = ons_ref[...].astype(F32)

    @pl.when(pl.program_id(0) == 0)
    def _():
        for k in range(nk + 1, width):
            rows_f[pl.ds(k, step_rows, stride=width), :] = jnp.zeros((step_rows, np_), F32)

    groups = step_rows // tied
    sample = lax.broadcasted_iota(jnp.int32, (np_, nt), 1)
    edge = jnp.minimum(sample, nt - sample).astype(F32)
    for g in range(groups):
        t = jnp.swapaxes(rows_f[pl.ds(g * 128, 128), :], 0, 1)
        col = t.astype(BF)
        for i in range(tied):
            x = g * tied + i
            update = dot(jnp.concatenate([col, col], 1), tab_ref[i], ((1,), (0,)))
            limit = t[:, i * width + nk:i * width + nk + 1]
            f = foc_ref[x].astype(F32)
            out_ref[x] = (f + jnp.where(edge < limit, update, 0.0)).astype(BF)


def shards(kernel, focus, onset):
    nf = lax.axis_size("freq")
    rows, np_, nt = focus.shape
    half = nf * rows
    table = forward_table(nt, nf)
    nk = 2 * nf
    table = table.reshape(nf, 2, nt).swapaxes(0, 1).reshape(nk, nt)
    fwd = jnp.asarray(np.concatenate(split(table), 0))
    inv_hi, inv_lo = split((table * np.float32(2.0 / nt)).astype(np.float32))
    width = 32
    while width < nk + 2:
        width *= 2
    tied = 128 // width
    right = np.zeros((tied, 256, nt), np.float32).astype(jnp.bfloat16)
    for i in range(tied):
        at = i * width
        right[i, at:at + nk] = inv_hi
        right[i, 128 + at:128 + at + nk] = inv_lo
    right = jnp.asarray(right)

    def vm(shape, kind=BF):
        return pltpu.VMEM(shape, kind)

    one = (nf, rows, np_)
    block = (2,) + one
    dma = pltpu.SemaphoreType.DMA
    spectra, own = pl.pallas_call(
        functools.partial(spectra_kernel, nf, rows, np_, nt),
        out_shape=[jax.ShapeDtypeStruct(block, BF), jax.ShapeDtypeStruct((rows, np_), jnp.int32)],
        in_specs=[pl.BlockSpec(memory_space=pl.ANY)] * 3 + [pl.BlockSpec(memory_space=pltpu.VMEM)],
        out_specs=[pl.BlockSpec(memory_space=pl.ANY)] * 2,
        scratch_shapes=[
            vm((2, 2 * half, half)), vm((rows, np_, nt)), vm((rows, np_), jnp.int32),
            vm((2, rows * nf, np_), F32),
            vm(block), vm(block), vm((2, 2 * half, np_), F32),
            vm(block), vm(block),
            vm(block), vm(block), vm(one, F32), vm((2, 4 * nf - 2, rows, np_), F32),
            vm(block), vm(block), vm(block), vm((2, np_, half), F32), vm(block),
            dma((NSUB + 2,)), dma((NSUB + 1, nf)), dma((NSUB + 1, nf)),
        ] + [dma((2, nf))] * 10,
        compiler_params=pltpu.CompilerParams(
            collective_id=0, has_side_effects=True, vmem_limit_bytes=58 << 20),
        cost_estimate=pl.CostEstimate(
            flops=32 * half * half * np_, bytes_accessed=8 * half * half, transcendentals=0),
    )(kernel, focus, onset, fwd)
    sr = min(rows, 32)
    return pl.pallas_call(
        functools.partial(final_kernel, nf, sr, width, np_, nt),
        out_shape=jax.ShapeDtypeStruct(focus.shape, BF),
        grid=(rows // sr,),
        in_specs=[
            pl.BlockSpec((2, nf, sr, np_), lambda i: (0, 0, i, 0)),
            pl.BlockSpec((sr, np_), lambda i: (i, 0)),
            pl.BlockSpec((sr, np_, nt), lambda i: (i, 0, 0)),
            pl.BlockSpec(right.shape, lambda i: (0, 0, 0)),
        ],
        out_specs=pl.BlockSpec((sr, np_, nt), lambda i: (i, 0, 0)),
        scratch_shapes=[pltpu.VMEM((sr * width, np_), F32)],
        compiler_params=pltpu.CompilerParams(vmem_limit_bytes=58 << 20),
    )(spectra, own, focus, right)


def solution(mesh):
    in_specs = (P("freq", None, None, "rcv"), P(("rcv", "freq"), "grp", None), P(None, "grp"))
    out_specs = P(("rcv", "freq"), "grp", None)
    return jax.shard_map(shards, mesh=mesh, in_specs=in_specs, out_specs=out_specs, check_vma=False)
```
